128 devices in a mesh: row: 16 (over y, z_hi, core), col: 8 (over x, z_lo).
Axes of the slice: x: 4, y: 4, z: 4 (z_hi: 2, z_lo: 2; z = z_hi * 2 + z_lo), core: 2. Of those that a mesh axis runs over, the one named last changes fastest.
Arguments:
- diag_block: float32 [512, 512], P('row', 'col'), may hold values from 0 to 2.5, as said below
- panel_below: float32 [49152, 512], P('row', 'col'), may hold values from -1.8 to 1.8
- trailing: float32 [49152, 6144], P('row', 'col'), may hold values from -6 to 6
Outputs:
- diag_factor: float32 [512, 512], P('row', 'col')
- panel_factor: float32 [49152, 512], P('row', 'col')
- new_trailing: float32 [49152, 6144], P('row', 'col')
The draws below stay inside these ranges and needn't reach their ends.
Inputs may be any that keep to these rules, and one draw needn't show every extreme that they name: `diag_block`: taken to matrix order in both dimensions, the block is symmetric with all eigenvalues 0.5 or more.
All inputs are finite; a program needn't handle non-finite values.
Results may differ from the reference program's by a relative error of at most 0.00015.
Values sent between devices are 32-bit elements; how exact they have to be, the bound alone decides.
No kernel may reach another device: no remote copies, remote signals or barrier semaphores. Data moves between devices by JAX's collectives and lax.ppermute only.
A program may use at most 128 MiB of HBM per device.

```python
import jax
import jax.numpy as jnp
from jax import lax

NB = 512
TC = 6144
BELOW = 49152
N_ROW = 16
N_COL = 8


def draw_diag_block(key, part):
    key_points, key_ridge = jax.random.split(key)
    points = jax.random.uniform(key_points, (NB, 3), jnp.float32, 0.0, 1.0)
    ridge = jax.random.uniform(key_ridge, (NB,), jnp.float32, 0.5, 1.5)
    index = jnp.arange(NB, dtype=jnp.int32)
    rows_block = NB // N_ROW
    cols_block = NB // N_COL
    row_map = index % rows_block * N_ROW + index // rows_block
    col_map = index % cols_block * N_COL + index // cols_block
    row_points = points[row_map]
    col_points = points[col_map]
    distance = jnp.zeros((NB, NB), jnp.float32)
    for coord in range(3):
        gap = row_points[:, coord][:, None] - col_points[:, coord][None, :]
        distance = distance + gap * gap
    length_scale = 0.6 / NB ** (1.0 / 3.0)
    kernel = jnp.exp(-distance / (2.0 * length_scale * length_scale))
    same = row_map[:, None] == col_map[None, :]
    kernel = kernel + jnp.where(same, ridge[row_map][:, None], 0.0)
    return kernel.astype(jnp.float32)


def level_of(key, dims, pieces, least, top_value):
    level = 1.0
    for position, blocks in pieces:
        heights = jax.random.uniform(jax.random.fold_in(jax.random.fold_in(key, 6), position), (blocks,), jnp.float32, least / len(pieces), top_value / len(pieces))
        level = level * jnp.repeat(jnp.exp(heights), dims[position] // blocks).reshape((-1,) + (1,) * (len(dims) - 1 - position))
    return level


def gaussian(stream_key, dims, width, reach, cuts=(), kind=jnp.bfloat16):
    level = level_of(stream_key, dims, cuts, -0.22, 0.18) if cuts else 1.0
    values = jax.random.normal(stream_key, dims, jnp.float32) * width * level
    return jnp.minimum(jnp.maximum(values, -reach), reach).astype(kind)


def setup_inputs(seed: int = 0) -> dict:
    arg_keys = jax.random.split(jax.random.key(seed), 4)
    diag_block = draw_diag_block(jax.random.fold_in(arg_keys[3], 71), 0)
    panel_below = gaussian(arg_keys[1], (BELOW, NB), 0.3, 1.8, ((0, 16), (1, 8)), jnp.float32)
    trailing = gaussian(arg_keys[2], (BELOW, TC), 1.0, 6.0, ((0, 16), (1, 8)), jnp.float32)
    return {"diag_block": diag_block, "panel_below": panel_below, "trailing": trailing}


def to_matrix(array, parts, axis):
    moved = jnp.moveaxis(array, axis, 0)
    length = moved.shape[0]
    shaped = moved.reshape((parts, length // parts) + moved.shape[1:])
    shaped = jnp.swapaxes(shaped, 0, 1).reshape(moved.shape)
    return jnp.moveaxis(shaped, 0, axis)

def to_storage(array, parts, axis):
    moved = jnp.moveaxis(array, axis, 0)
    length = moved.shape[0]
    shaped = moved.reshape((length // parts, parts) + moved.shape[1:])
    shaped = jnp.swapaxes(shaped, 0, 1).reshape(moved.shape)
    return jnp.moveaxis(shaped, 0, axis)

def reference(diag_block, panel_below, trailing):
    diag_matrix = to_matrix(to_matrix(diag_block, N_ROW, 0), N_COL, 1)
    factor = jnp.linalg.cholesky(diag_matrix)
    diag_factor = to_storage(to_storage(factor, N_ROW, 0), N_COL, 1)
    identity = jnp.eye(NB, dtype=jnp.float32)
    inverse = lax.linalg.triangular_solve(factor, identity, left_side=True, lower=True)
    panel_matrix = to_matrix(panel_below, N_COL, 1)
    solved = jnp.dot(panel_matrix.astype(jnp.float32), inverse.T.astype(jnp.float32), precision=lax.Precision.HIGHEST, preferred_element_type=jnp.float32)
    panel_factor = to_storage(solved, N_COL, 1)
    solved_matrix = to_matrix(solved, N_ROW, 0)
    top_store = to_storage(solved_matrix[:TC], N_COL, 0)
    update = jnp.dot(solved.astype(jnp.float32), top_store.T.astype(jnp.float32), precision=lax.Precision.HIGHEST, preferred_element_type=jnp.float32)
    new_trailing = trailing - update
    return (diag_factor, panel_factor, new_trailing)
```

```python
import functools

import jax
import jax.numpy as jnp
from jax import lax
from jax.experimental import pallas as pl
from jax.experimental.pallas import tpu as pltpu
from jax.sharding import Mesh
from jax.sharding import PartitionSpec as P

HI = lax.Precision.HIGHEST
WIDTH = 512
BLK = 128
SUB = 8


def dot(a, b, ca, cb, precision=HI):
    return lax.dot_general(
        a, b, (((ca,), (cb,)), ((), ())), precision=precision, preferred_element_type=jnp.float32
    )


def eliminate(rows):
    count = len(rows)
    lane = lax.broadcasted_iota(jnp.int32, (SUB, BLK), 1)
    sub = lax.broadcasted_iota(jnp.int32, (SUB, BLK), 0)
    rows = list(rows)
    scales = []
    for b in range(count):
        cols = {
            i: [
                jnp.broadcast_to(rows[i][:, SUB * b + k : SUB * b + k + 1], (SUB, BLK))
                for k in range(SUB)
            ]
            for i in range(b, count)
        }
        scale = jnp.zeros((SUB, BLK), jnp.float32)
        for j in range(SUB):
            pivot_row = {
                k: jnp.broadcast_to(cols[b][k][j : j + 1, :], (SUB, BLK)) for k in range(j, SUB)
            }
            at = lane == SUB * b + j
            wide = jnp.where(at, 1.0, jnp.broadcast_to(rows[b][j : j + 1, :], (SUB, BLK)))
            inv = 1.0 / pivot_row[j]
            scale = jnp.where(sub == j, lax.rsqrt(pivot_row[j]), scale)
            for i in range(b, count):
                m = cols[i][j] * inv
                here = at
                if i == b:
                    m = jnp.where(sub > j, m, 0.0)
                    here = at & (sub > j)
                for k in range(j + 1, SUB):
                    cols[i][k] = cols[i][k] - m * pivot_row[k]
                rows[i] = jnp.where(here, 0.0, rows[i]) - m * wide
        rows[b] = rows[b] * scale
        scales.append(scale)
    return rows, scales


def factor_kernel(a_ref, u_ref, m_ref, r_ref, t_ref):
    lane = lax.broadcasted_iota(jnp.int32, (SUB, BLK), 1)
    sub = lax.broadcasted_iota(jnp.int32, (SUB, BLK), 0)
    r_ref[...] = a_ref[...]
    u_ref[...] = jnp.zeros_like(u_ref)
    m_ref[...] = jnp.zeros_like(m_ref)
    for o in range(0, WIDTH, BLK):
        e = o + BLK
        rows = [r_ref[o + i : o + i + SUB, o:e] for i in range(0, BLK, SUB)]
        rows, scales = eliminate(rows)
        for i in range(BLK // SUB):
            at = sub + SUB * i
            u_ref[o + SUB * i : o + SUB * i + SUB, o:e] = jnp.where(lane >= at, rows[i], 0.0)
            t_ref[SUB * i : SUB * i + SUB, :] = jnp.where(
                lane < at, rows[i], jnp.where(lane == at, scales[i], 0.0)
            )
        inv = t_ref[...]
        m_ref[o:e, o:e] = inv
        if o:
            m_ref[o:e, :o] = dot(inv, r_ref[o:e, :o], 1, 0)
        if e < WIDTH:
            u = dot(inv, r_ref[o:e, e:], 1, 0)
            u_ref[o:e, e:] = u
            r_ref[e:, e:] = r_ref[e:, e:] - dot(u, u, 0, 0)
            z = dot(u, m_ref[o:e, :e], 0, 0)
            if o:
                r_ref[e:, :o] = r_ref[e:, :o] - z[:, :o]
            r_ref[e:, o:e] = -z[:, o:]


def factor_and_inverse(a):
    whole = pl.BlockSpec(memory_space=pltpu.VMEM)
    return pl.pallas_call(
        factor_kernel,
        out_shape=[jax.ShapeDtypeStruct((WIDTH, WIDTH), jnp.float32)] * 2,
        in_specs=[whole],
        out_specs=[whole] * 2,
        scratch_shapes=[
            pltpu.VMEM((WIDTH, WIDTH), jnp.float32),
            pltpu.VMEM((BLK, BLK), jnp.float32),
        ],
        cost_estimate=pl.CostEstimate(flops=2 * 10**10, bytes_accessed=10**6, transcendentals=0),
        compiler_params=pltpu.CompilerParams(vmem_limit_bytes=16 << 20),
    )(a)


def ring(n, step):
    return [(i, (i + step) % n) for i in range(n)]


def shift(x, axis, step):
    return lax.ppermute(x, axis, ring(lax.axis_size(axis), step))


def order(*arrays):
    return lax.optimization_barrier(arrays)


def gather_diag(tile):
    half = tile.shape[0] // 2
    flat = jnp.concatenate([tile[:half], tile[half:]], axis=1)
    mine = lax.all_to_all(
        jnp.broadcast_to(flat[None], (64,) + flat.shape), ("y", "zh", "x", "zl"), 0, 0, tiled=True
    )
    other = shift(mine, "core", 1)
    first = lax.axis_index("core") == 0
    return jnp.stack([jnp.where(first, mine, other), jnp.where(first, other, mine)])


def shards(diag_block, panel_below, trailing):
    y, zh, core = lax.axis_index("y"), lax.axis_index("zh"), lax.axis_index("core")
    x, zl = lax.axis_index("x"), lax.axis_index("zl")
    panel_t = panel_below.T
    top_len = trailing.shape[1] // 2
    perm = []
    for src in range(128):
        yy, zz, cc, xx, ll = src // 32, src // 16 % 2, src // 8 % 2, src // 2 % 4, src % 2
        dy, dz, dc = xx, ll, yy // 2
        dx, dl = 2 * (yy % 2) + zz, cc
        perm.append((src, (((dy * 2 + dz) * 2 + dc) * 4 + dx) * 2 + dl))
    piece = lax.ppermute(panel_t[:, :top_len], ("y", "zh", "core", "x", "zl"), perm)
    from_z = shift(panel_t, "zl", 1)
    from_l = shift(panel_t, "x", 1)
    from_r = shift(panel_t, "x", -1)
    tiles = gather_diag(diag_block)
    piece_z = shift(piece, "zh", 1)
    z_first = zh == 0
    pair = jnp.stack([jnp.where(z_first, piece, piece_z), jnp.where(z_first, piece_z, piece)])
    pairs = [pair] + [shift(pair, "y", s) for s in (1, 2, 3)]
    tiles = tiles.reshape(2, 4, 2, 4, 2, 16, 2, 64)
    diag = tiles.transpose(6, 5, 1, 2, 0, 7, 3, 4).reshape(WIDTH, WIDTH)
    diag, from_z, from_l, from_r = order(diag, from_z, from_l, from_r)
    from_rz = shift(from_r, "zl", 1)
    from_lz = shift(from_z, "x", 1)
    from_2 = shift(from_r, "x", -1)
    upper, inverse = factor_and_inverse(diag)
    upper, inverse, from_rz, from_lz, from_2, *pairs = order(
        upper, inverse, from_rz, from_lz, from_2, *pairs
    )
    third = panel_t.shape[1] // 3
    part_a = shift(from_2[:, :third], "zl", 1)
    part_b = shift(from_lz[:, third : 2 * third], "x", 1)
    part_c = shift(from_rz[:, 2 * third :], "x", -1)
    from_2z = jnp.concatenate([part_a, part_b, part_c], axis=1)
    slots = jnp.stack(pairs)
    slots = jnp.concatenate([lax.dynamic_index_in_dim(slots, (y - i) % 4, 0) for i in range(4)])
    own_half = slots.reshape(WIDTH, top_len)
    other_half = shift(own_half, "core", 1)
    c_first = core == 0
    even = jnp.where(c_first, own_half, other_half)
    odd = jnp.where(c_first, other_half, own_half)
    top_t = jnp.stack([even, odd], axis=2).reshape(WIDTH, 2 * top_len)
    inv3 = inverse.reshape(WIDTH, 64, 8)
    inv_store = inv3.transpose(0, 2, 1).reshape(WIDTH, WIDTH)
    solved_top = dot(inv_store, top_t, 1, 0)
    def place(dx, dz):
        return ((x + dx) % 4) * 2 + (zl + dz) % 2

    blocks = [panel_t, from_z, from_l, from_r, from_rz, from_lz, from_2, from_2z]
    places = [(0, 0), (0, 1), (3, 0), (1, 0), (1, 1), (3, 1), (2, 0), (2, 1)]
    inv_arrived = jnp.concatenate(
        [
            lax.dynamic_slice_in_dim(inv_store, place(*p) * 64, 64, axis=1)
            for p in places
        ],
        axis=1,
    )
    weights = dot(inv_arrived, solved_top, 0, 0)
    gathered = jnp.concatenate(blocks, axis=0)
    col = x * 2 + zl
    row = (y * 2 + zh) * 2 + core
    inv_rows = lax.dynamic_index_in_dim(inv_arrived.reshape(64, 8, WIDTH), col, 1, False)
    panel_factor = dot(inv_rows, gathered, 1, 0, lax.Precision.HIGH).T
    factor_cols = lax.dynamic_index_in_dim(upper.reshape(64, 8, WIDTH), col, 1, False)
    diag_factor = lax.dynamic_index_in_dim(factor_cols.T.reshape(32, 16, 64), row, 1, False)
    new_trailing = trailing - dot(gathered, weights, 0, 0, lax.Precision.HIGH)
    return (diag_factor, panel_factor, new_trailing)


def solution(mesh):
    fine = Mesh(mesh.devices.reshape(4, 2, 2, 4, 2), ("y", "zh", "core", "x", "zl"))
    spec = P(("y", "zh", "core"), ("x", "zl"))
    return jax.shard_map(
        shards, mesh=fine, in_specs=(spec,) * 3, out_specs=(spec,) * 3, check_vma=False
    )
```

```python
import functools

import jax
import jax.numpy as jnp
from jax import lax
from jax.experimental import pallas as pl
from jax.experimental.pallas import tpu as pltpu
from jax.sharding import Mesh
from jax.sharding import PartitionSpec as P

HI = lax.Precision.HIGHEST
WIDTH = 512
BLK = 128
SUB = 8


def dot(a, b, ca, cb, precision=HI):
    return lax.dot_general(
        a, b, (((ca,), (cb,)), ((), ())), precision=precision, preferred_element_type=jnp.float32
    )


def lanes_of(x, k):
    return jnp.broadcast_to(x[:, k : k + 1], (SUB, BLK))


def row_of(x, j):
    return jnp.broadcast_to(x[j : j + 1, :], (SUB, BLK))


def eliminate_strip(rows, first):
    lane = lax.broadcasted_iota(jnp.int32, (SUB, BLK), 1)
    sub = lax.broadcasted_iota(jnp.int32, (SUB, BLK), 0)
    rows, scales, ahead = list(rows), [], None
    for b in range(len(rows)):
        base = SUB * (first + b)
        cols = {
            i: [lanes_of(rows[i], base + k) for k in range(SUB)]
            for i in range(b, len(rows))
            if i > b or ahead is None
        }
        if ahead is not None:
            cols[b] = ahead
        if b + 1 < len(rows):
            ahead = [lanes_of(rows[b + 1], base + SUB + k) for k in range(SUB)]
        scale = jnp.zeros((SUB, BLK), jnp.float32)
        for j in range(SUB):
            pivot_row = {k: row_of(cols[b][k], j) for k in range(j, SUB)}
            at = lane == base + j
            wide = jnp.where(at, 1.0, row_of(rows[b], j))
            inv = 1.0 / pivot_row[j]
            scale = jnp.where(sub == j, lax.rsqrt(pivot_row[j]), scale)
            for i in range(b, len(rows)):
                m = cols[i][j] * inv
                here = at
                if i == b:
                    m = jnp.where(sub > j, m, 0.0)
                    here = at & (sub > j)
                if i == b + 1:
                    for k in range(SUB):
                        ahead[k] = ahead[k] - m * row_of(cols[i][j], k)
                for k in range(j + 1, SUB):
                    cols[i][k] = cols[i][k] - m * pivot_row[k]
                rows[i] = jnp.where(here, 0.0, rows[i]) - m * wide
        rows[b] = rows[b] * scale
        scales.append(scale)
    return rows, scales


def eliminate(rows, strip=8):
    lane = lax.broadcasted_iota(jnp.int32, (SUB, BLK), 1)
    sub = lax.broadcasted_iota(jnp.int32, (SUB, BLK), 0)
    rows, scales = list(rows), []
    for s in range(0, len(rows), strip):
        e = s + strip
        rows[s:e], found = eliminate_strip(rows[s:e], s)
        scales += found
        if e < len(rows):
            inside = (lane >= SUB * s) & (lane < SUB * e)
            own = [
                jnp.where(
                    inside & (lane >= sub + SUB * i),
                    jnp.where(lane == sub + SUB * i, scales[i], 0.0),
                    rows[i],
                )
                for i in range(s, e)
            ]
            change = dot(jnp.concatenate(rows[s:e], axis=0), jnp.concatenate(own, axis=0), 0, 0)
            for i in range(e, len(rows)):
                rows[i] = jnp.where(inside, 0.0, rows[i]) - change[SUB * i : SUB * i + SUB]
    return rows, scales


def fill(tall_ref, start, stride, value):
    rows, columns = value.shape
    height = tall_ref.shape[0] * BLK // columns
    for i in range(columns // BLK):
        tall_ref[pl.ds(i * height + start, rows, stride=stride), :] = value[:, BLK * i : BLK * i + BLK]


def pick(tall_ref, start, stride, rows, columns, height):
    return jnp.concatenate(
        [
            tall_ref[pl.ds(i * height + start, rows, stride=stride), :]
            for i in range(columns // BLK)
        ],
        axis=1,
    )


def lay(tall_ref, value):
    height = value.shape[0]
    for i in range(value.shape[1] // BLK):
        tall_ref[i * height : i * height + height, :] = value[:, BLK * i : BLK * i + BLK]


def assemble(mine_ref, other_ref, wide_ref, tall_ref, a_ref):
    core = lax.axis_index("core")
    left = lax.broadcasted_iota(jnp.int32, (16, BLK), 1) < BLK // 2
    for ref, start in ((mine_ref, core), (other_ref, 1 - core)):
        for yz in range(8):
            for x in range(4):
                one, two = ref[yz * 8 + 2 * x], ref[yz * 8 + 2 * x + 1]
                upper = jnp.where(left, one, pltpu.roll(two, BLK // 2, 1))
                lower = jnp.where(left, pltpu.roll(one, BLK // 2, 1), two)
                at = x * WIDTH + yz * 2 + start
                wide_ref[pl.ds(at, 16, stride=16), :] = upper
                wide_ref[pl.ds(at + WIDTH // 2, 16, stride=16), :] = lower
    for x in range(4):
        turned = wide_ref[x * WIDTH : x * WIDTH + WIDTH, :].T
        fill(tall_ref, 2 * x, 8, turned[:64])
        fill(tall_ref, 2 * x + 1, 8, turned[64:])
    for i in range(4):
        a_ref[:, BLK * i : BLK * i + BLK] = tall_ref[i * WIDTH : i * WIDTH + WIDTH, :]


def factor_steps(offsets, r_ref, u_ref, m_ref, t_ref):
    lane = lax.broadcasted_iota(jnp.int32, (SUB, BLK), 1)
    sub = lax.broadcasted_iota(jnp.int32, (SUB, BLK), 0)
    for o in offsets:
        e = o + BLK
        rows = [r_ref[o + i : o + i + SUB, o:e] for i in range(0, BLK, SUB)]
        rows, scales = eliminate(rows)
        for i in range(BLK // SUB):
            at = sub + SUB * i
            u_ref[o + SUB * i : o + SUB * i + SUB, o:e] = jnp.where(lane >= at, rows[i], 0.0)
            t_ref[SUB * i : SUB * i + SUB, :] = jnp.where(
                lane < at, rows[i], jnp.where(lane == at, scales[i], 0.0)
            )
        inv = t_ref[...]
        m_ref[o:e, o:e] = inv
        if o:
            m_ref[o:e, :o] = dot(inv, r_ref[o:e, :o], 1, 0)
        if e < WIDTH:
            u = dot(inv, r_ref[o:e, e:], 1, 0)
            u_ref[o:e, e:] = u
            r_ref[e:, e:] = r_ref[e:, e:] - dot(u, u, 0, 0)
            z = dot(u, m_ref[o:e, :e], 0, 0)
            if o:
                r_ref[e:, :o] = r_ref[e:, :o] - z[:, :o]
            r_ref[e:, o:e] = -z[:, o:]


VMEM = pl.BlockSpec(memory_space=pltpu.VMEM)


def cost(flops, bytes_accessed):
    return pl.CostEstimate(flops=flops, bytes_accessed=bytes_accessed, transcendentals=0)


PLACES = ((0, 0), (0, 1), (3, 0), (1, 0), (1, 1), (3, 1), (2, 0), (2, 1))


def weights_kernel(
    mine_ref, other_ref, p0_ref, p1_ref, p2_ref, p3_ref, d_ref, own_ref, w_ref,
    r_ref, u_ref, m_ref, b_ref, wide_ref, t_ref, k_ref, p_ref,
):
    assemble(mine_ref, other_ref, wide_ref, t_ref, r_ref)
    u_ref[...] = jnp.zeros_like(u_ref)
    m_ref[...] = jnp.zeros_like(m_ref)
    factor_steps(range(0, WIDTH, BLK), r_ref, u_ref, m_ref, b_ref)
    y, zh, core = lax.axis_index("y"), lax.axis_index("zh"), lax.axis_index("core")
    x, zl = lax.axis_index("x"), lax.axis_index("zl")
    col, row = x * 2 + zl, (y * 2 + zh) * 2 + core
    half = WIDTH // 8
    lay(t_ref, m_ref[...].T)
    arrived = [2 * ((x + dx) % 4) + (zl + dz) % 2 for dx, dz in PLACES]
    for i in range(8):
        c = 2 * ((y + 4 - i // 2) % 4) + (zh + i % 2) % 2
        k_ref[half * i : half * i + half, :] = pick(t_ref, c, 8, half, WIDTH, WIDTH)
    for i, c in enumerate(arrived):
        p_ref[half * i : half * i + half, :] = pick(t_ref, c, 8, half, WIDTH, WIDTH)
    top = jnp.concatenate(
        [ref[i] for ref in (p0_ref, p1_ref, p2_ref, p3_ref) for i in range(2)], axis=0
    )
    solved = dot(top, k_ref[...], 0, 0)
    w_ref[...] = dot(solved, p_ref[...], 1, 1)
    lay(t_ref, m_ref[...])
    mine = pick(t_ref, col, 8, half, WIDTH, WIDTH)
    lay(t_ref, u_ref[...])
    both = jnp.concatenate([mine, pick(t_ref, col, 8, half, WIDTH, WIDTH)], axis=0).T
    t_ref[:WIDTH, :] = both
    own = jnp.concatenate([t_ref[pl.ds(c, half, stride=8), :] for c in arrived], axis=0)
    own_ref[...] = own[:, :half].T
    d_ref[...] = t_ref[pl.ds(row, WIDTH // 16, stride=16), :][:, half:]


def make_weights(mine, other, pairs):
    square, tall = pltpu.VMEM((WIDTH, WIDTH), jnp.float32), pltpu.VMEM((4 * WIDTH, BLK), jnp.float32)
    return pl.pallas_call(
        weights_kernel,
        out_shape=[
            jax.ShapeDtypeStruct((WIDTH // 16, WIDTH // 8), jnp.float32),
            jax.ShapeDtypeStruct((WIDTH // 8, WIDTH), jnp.float32),
            jax.ShapeDtypeStruct((pairs[0].shape[2], WIDTH), jnp.float32),
        ],
        in_specs=[VMEM] * 6,
        out_specs=[VMEM] * 3,
        scratch_shapes=[square] * 3
        + [pltpu.VMEM((BLK, BLK), jnp.float32), tall, tall, square, square],
        cost_estimate=cost(3 * 10**10, 10**6),
        compiler_params=pltpu.CompilerParams(vmem_limit_bytes=24 << 20),
        name="weights",
    )(mine, other, *pairs)


def split(a):
    high = a.astype(jnp.bfloat16)
    return high, (a - high.astype(jnp.float32)).astype(jnp.bfloat16)


def thrice(a, b, ca, cb):
    (ah, al), (bh, bl) = a, b
    return dot(ah, bh, ca, cb, None) + dot(ah, bl, ca, cb, None) + dot(al, bh, ca, cb, None)


def subtract(place, own, high, low, blocks, trail_ref, pf, pf_ref, out_ref):
    part = jnp.concatenate([ref[...] for ref in blocks], axis=0)
    at = slice(WIDTH // 8 * place, WIDTH // 8 * place + part.shape[0])
    mine = thrice(split(own[:, at]), split(part), 1, 0)
    pf_ref[...] = mine if pf is None else pf[...] + mine
    (ah, al), bh, bl = split(part.T), high[at, :], low[at, :]
    if 3 * part.shape[0] <= 256:
        change = dot(
            jnp.concatenate([ah, al, ah], axis=1), jnp.concatenate([bh, bh, bl], axis=0), 1, 0, None
        )
    else:
        change = thrice((ah, al), (bh, bl), 1, 0)
    out_ref[...] = trail_ref[...] - change


def start_kernel(mine_ref, other_ref, own_ref, *refs):
    blocks, (trail_ref, pf_ref, out_ref, high_ref, low_ref, w_ref) = refs[:-6], refs[-6:]

    @pl.when(pl.program_id(0) == 0)
    def _():
        core = lax.axis_index("core")
        n = mine_ref.shape[0]
        fill(w_ref, core, 2, mine_ref[...])
        fill(w_ref, 1 - core, 2, other_ref[...])
        for i in range(WIDTH // BLK):
            at = slice(BLK * i, BLK * i + BLK)
            high_ref[at, :], low_ref[at, :] = split(w_ref[2 * n * i : 2 * n * i + 2 * n, :].T)

    subtract(0, own_ref[...], high_ref, low_ref, blocks, trail_ref, None, pf_ref, out_ref)


def go_on_kernel(own_ref, high_ref, low_ref, *refs, place):
    blocks, (pf_in_ref, trail_ref, pf_ref, out_ref) = refs[:-4], refs[-4:]
    subtract(place, own_ref[...], high_ref, low_ref, blocks, trail_ref, pf_in_ref, pf_ref, out_ref)


def whole(shape):
    return pl.BlockSpec(shape, lambda i: (0, 0))


def update_start(mine, other, own, blocks, trailing, tile=256):
    rows, columns = trailing.shape
    lanes = pl.BlockSpec((WIDTH // 8, tile), lambda i: (0, i))
    wide = pl.BlockSpec((tile, columns), lambda i: (i, 0))
    return pl.pallas_call(
        start_kernel,
        grid=(rows // tile,),
        out_shape=[
            jax.ShapeDtypeStruct((WIDTH // 8, rows), jnp.float32),
            jax.ShapeDtypeStruct((rows, columns), jnp.float32),
        ]
        + [jax.ShapeDtypeStruct((WIDTH, columns), jnp.bfloat16)] * 2,
        in_specs=[whole(mine.shape), whole(other.shape), whole(own.shape)] + [lanes] * len(blocks)
        + [wide],
        out_specs=[lanes, wide] + [whole((WIDTH, columns))] * 2,
        scratch_shapes=[pltpu.VMEM((columns * WIDTH // BLK, BLK), jnp.float32)],
        cost_estimate=cost(8 * 10**9, 10**7),
        compiler_params=pltpu.CompilerParams(vmem_limit_bytes=20 << 20),
        name="update_start",
    )(mine, other, own, *blocks, trailing)


def update_more(place, own, high, low, blocks, pf, trailing, tile, name):
    rows, columns = trailing.shape
    lanes = pl.BlockSpec((WIDTH // 8, tile), lambda i: (0, i))
    wide = pl.BlockSpec((tile, columns), lambda i: (i, 0))
    return pl.pallas_call(
        functools.partial(go_on_kernel, place=place),
        grid=(rows // tile,),
        out_shape=[
            jax.ShapeDtypeStruct((WIDTH // 8, rows), jnp.float32),
            jax.ShapeDtypeStruct((rows, columns), jnp.float32),
        ],
        in_specs=[whole(own.shape), whole(high.shape), whole(low.shape)]
        + [lanes] * (len(blocks) + 1)
        + [wide],
        out_specs=[lanes, wide],
        cost_estimate=cost(10**9 * len(blocks), 10**7),
        compiler_params=pltpu.CompilerParams(vmem_limit_bytes=16 << 20),
        name=name,
    )(own, high, low, *blocks, pf, trailing)


def ring(n, step):
    return [(i, (i + step) % n) for i in range(n)]


def shift(x, axis, step):
    return lax.ppermute(x, axis, ring(lax.axis_size(axis), step))


def order(*arrays):
    return lax.optimization_barrier(arrays)


def gather_tiles(tile):
    half = tile.shape[0] // 2
    flat = jnp.concatenate([tile[:half], tile[half:]], axis=1)
    return lax.all_to_all(
        jnp.broadcast_to(flat[None], (64,) + flat.shape), ("y", "zh", "x", "zl"), 0, 0, tiled=True
    )


def top_moves(flip):
    moves = []
    for source in range(128):
        y, zh, core, x, zl = (source // s % n for s, n in ((32, 4), (16, 2), (8, 2), (2, 4), (1, 2)))
        target = (((x * 2 + (zl + flip) % 2) * 2 + y // 2) * 4 + 2 * (y % 2) + zh) * 2 + core
        moves.append((source, target))
    return moves


def shards(diag_block, panel_below, trailing):
    panel_t = panel_below.T
    top_len = trailing.shape[1] // 2
    everything = ("y", "zh", "core", "x", "zl")
    raw = panel_t[:, :top_len]
    pieces = [lax.ppermute(raw, everything, top_moves(flip)) for flip in (0, 1)]
    diag_block, *pieces = order(diag_block, *pieces)
    from_z = shift(panel_t, "zl", 1)
    from_l = shift(panel_t, "x", 1)
    from_r = shift(panel_t, "x", -1)
    mine = gather_tiles(diag_block)
    head = BLK
    ahead = shift(from_r[:, :head], "x", -1)
    ahead, *pieces = order(ahead, *pieces)
    pair = jnp.stack(pieces)
    pairs = [pair] + [shift(pair, "y", s) for s in (1, 2, 3)]
    other = shift(mine, "core", 1)
    mine, other, from_z, from_l, from_r, ahead = order(mine, other, from_z, from_l, from_r, ahead)
    from_rz = shift(from_r, "zl", 1)
    from_lz = shift(from_z, "x", 1)
    from_2 = jnp.concatenate([ahead, shift(from_r[:, head:], "x", -1)], axis=1)
    diag_factor, own, weights = make_weights(mine, other, pairs)
    weights, from_rz, from_lz, from_2 = order(weights, from_rz, from_lz, from_2)
    weights_other = shift(weights, "core", 1)
    third = panel_t.shape[1] // 3
    parts = (
        shift(from_2[:, :third], "zl", 1),
        shift(from_lz[:, third : 2 * third], "x", 1),
        shift(from_rz[:, 2 * third :], "x", -1),
    )
    blocks = [panel_t, from_z, from_l, from_r, from_rz, from_lz, from_2]
    factor_part, rest, high, low = update_start(weights, weights_other, own, blocks, trailing)
    factor_part, rest, *parts = order(factor_part, rest, *parts)
    from_2z = jnp.concatenate(parts, axis=1)
    panel_factor, new_trailing = update_more(
        7, own, high, low, [from_2z], factor_part, rest, 512, "update_last"
    )
    return (diag_factor, panel_factor.T, new_trailing)


def solution(mesh):
    fine = Mesh(mesh.devices.reshape(4, 2, 2, 4, 2), ("y", "zh", "core", "x", "zl"))
    spec = P(("y", "zh", "core"), ("x", "zl"))
    return jax.shard_map(
        shards, mesh=fine, in_specs=(spec,) * 3, out_specs=(spec,) * 3, check_vma=False
    )
```

```python
import functools

import jax
import jax.numpy as jnp
from jax import lax
from jax.experimental import pallas as pl
from jax.experimental.pallas import tpu as pltpu
from jax.sharding import Mesh
from jax.sharding import PartitionSpec as P

HI = lax.Precision.HIGHEST
WIDTH = 512
BLK = 128
SUB = 8


def dot(a, b, ca, cb, precision=HI):
    return lax.dot_general(
        a, b, (((ca,), (cb,)), ((), ())), precision=precision, preferred_element_type=jnp.float32
    )


def lanes_of(x, k):
    return jnp.broadcast_to(x[:, k : k + 1], (SUB, BLK))


def row_of(x, j):
    return jnp.broadcast_to(x[j : j + 1, :], (SUB, BLK))


def eliminate_strip(rows, first):
    lane = lax.broadcasted_iota(jnp.int32, (SUB, BLK), 1)
    sub = lax.broadcasted_iota(jnp.int32, (SUB, BLK), 0)
    rows, scales, ahead = list(rows), [], None
    for b in range(len(rows)):
        base = SUB * (first + b)
        cols = {
            i: [lanes_of(rows[i], base + k) for k in range(SUB)]
            for i in range(b, len(rows))
            if i > b or ahead is None
        }
        if ahead is not None:
            cols[b] = ahead
        if b + 1 < len(rows):
            ahead = [lanes_of(rows[b + 1], base + SUB + k) for k in range(SUB)]
        scale = jnp.zeros((SUB, BLK), jnp.float32)
        for j in range(SUB):
            pivot_row = {k: row_of(cols[b][k], j) for k in range(j, SUB)}
            at = lane == base + j
            wide = jnp.where(at, 1.0, row_of(rows[b], j))
            inv = 1.0 / pivot_row[j]
            scale = jnp.where(sub == j, lax.rsqrt(pivot_row[j]), scale)
            for i in range(b, len(rows)):
                m = cols[i][j] * inv
                here = at
                if i == b:
                    m = jnp.where(sub > j, m, 0.0)
                    here = at & (sub > j)
                if i == b + 1:
                    for k in range(SUB):
                        ahead[k] = ahead[k] - m * row_of(cols[i][j], k)
                for k in range(j + 1, SUB):
                    cols[i][k] = cols[i][k] - m * pivot_row[k]
                rows[i] = jnp.where(here, 0.0, rows[i]) - m * wide
        rows[b] = rows[b] * scale
        scales.append(scale)
    return rows, scales


def eliminate(rows, strip=8):
    lane = lax.broadcasted_iota(jnp.int32, (SUB, BLK), 1)
    sub = lax.broadcasted_iota(jnp.int32, (SUB, BLK), 0)
    rows, scales = list(rows), []
    for s in range(0, len(rows), strip):
        e = s + strip
        rows[s:e], found = eliminate_strip(rows[s:e], s)
        scales += found
        if e < len(rows):
            inside = (lane >= SUB * s) & (lane < SUB * e)
            own = [
                jnp.where(
                    inside & (lane >= sub + SUB * i),
                    jnp.where(lane == sub + SUB * i, scales[i], 0.0),
                    rows[i],
                )
                for i in range(s, e)
            ]
            change = dot(jnp.concatenate(rows[s:e], axis=0), jnp.concatenate(own, axis=0), 0, 0)
            for i in range(e, len(rows)):
                rows[i] = jnp.where(inside, 0.0, rows[i]) - change[SUB * i : SUB * i + SUB]
    return rows, scales


def fill(tall_ref, start, stride, value):
    rows, columns = value.shape
    height = tall_ref.shape[0] * BLK // columns
    for i in range(columns // BLK):
        tall_ref[pl.ds(i * height + start, rows, stride=stride), :] = value[:, BLK * i : BLK * i + BLK]


def pick(tall_ref, start, stride, rows, columns, height):
    return jnp.concatenate(
        [
            tall_ref[pl.ds(i * height + start, rows, stride=stride), :]
            for i in range(columns // BLK)
        ],
        axis=1,
    )


def lay(tall_ref, value):
    height = value.shape[0]
    for i in range(value.shape[1] // BLK):
        tall_ref[i * height : i * height + height, :] = value[:, BLK * i : BLK * i + BLK]


def assemble(mine_ref, other_ref, wide_ref, tall_ref, a_ref):
    core = lax.axis_index("core")
    left = lax.broadcasted_iota(jnp.int32, (16, BLK), 1) < BLK // 2
    for ref, start in ((mine_ref, core), (other_ref, 1 - core)):
        for yz in range(8):
            for x in range(4):
                one, two = ref[yz * 8 + 2 * x], ref[yz * 8 + 2 * x + 1]
                upper = jnp.where(left, one, pltpu.roll(two, BLK // 2, 1))
                lower = jnp.where(left, pltpu.roll(one, BLK // 2, 1), two)
                at = x * WIDTH + yz * 2 + start
                wide_ref[pl.ds(at, 16, stride=16), :] = upper
                wide_ref[pl.ds(at + WIDTH // 2, 16, stride=16), :] = lower
    for x in range(4):
        turned = wide_ref[x * WIDTH : x * WIDTH + WIDTH, :].T
        fill(tall_ref, 2 * x, 8, turned[:64])
        fill(tall_ref, 2 * x + 1, 8, turned[64:])
    for i in range(4):
        a_ref[:, BLK * i : BLK * i + BLK] = tall_ref[i * WIDTH : i * WIDTH + WIDTH, :]


def factor_steps(offsets, r_ref, u_ref, m_ref, t_ref):
    lane = lax.broadcasted_iota(jnp.int32, (SUB, BLK), 1)
    sub = lax.broadcasted_iota(jnp.int32, (SUB, BLK), 0)
    for o in offsets:
        e = o + BLK
        rows = [r_ref[o + i : o + i + SUB, o:e] for i in range(0, BLK, SUB)]
        rows, scales = eliminate(rows)
        for i in range(BLK // SUB):
            at = sub + SUB * i
            u_ref[o + SUB * i : o + SUB * i + SUB, o:e] = jnp.where(lane >= at, rows[i], 0.0)
            t_ref[SUB * i : SUB * i + SUB, :] = jnp.where(
                lane < at, rows[i], jnp.where(lane == at, scales[i], 0.0)
            )
        inv = t_ref[...]
        m_ref[o:e, o:e] = inv
        if o:
            m_ref[o:e, :o] = dot(inv, r_ref[o:e, :o], 1, 0)
        if e < WIDTH:
            u = dot(inv, r_ref[o:e, e:], 1, 0)
            u_ref[o:e, e:] = u
            r_ref[e:, e:] = r_ref[e:, e:] - dot(u, u, 0, 0)
            z = dot(u, m_ref[o:e, :e], 0, 0)
            if o:
                r_ref[e:, :o] = r_ref[e:, :o] - z[:, :o]
            r_ref[e:, o:e] = -z[:, o:]


def first_half_kernel(mine_ref, other_ref, r_ref, u_ref, m_ref, t_ref, wide_ref, tall_ref):
    assemble(mine_ref, other_ref, wide_ref, tall_ref, r_ref)
    u_ref[...] = jnp.zeros_like(u_ref)
    m_ref[...] = jnp.zeros_like(m_ref)
    factor_steps((0, BLK), r_ref, u_ref, m_ref, t_ref)


def second_half_kernel(r_in, u_in, m_in, r_ref, u_ref, m_ref, t_ref):
    del r_in, u_in, m_in
    factor_steps((2 * BLK, 3 * BLK), r_ref, u_ref, m_ref, t_ref)


VMEM = pl.BlockSpec(memory_space=pltpu.VMEM)


def cost(flops, bytes_accessed):
    return pl.CostEstimate(flops=flops, bytes_accessed=bytes_accessed, transcendentals=0)


SQUARES = [jax.ShapeDtypeStruct((WIDTH, WIDTH), jnp.float32)] * 3


def factor_first(mine, other):
    return pl.pallas_call(
        first_half_kernel,
        out_shape=SQUARES,
        in_specs=[VMEM] * 2,
        out_specs=[VMEM] * 3,
        scratch_shapes=[
            pltpu.VMEM((BLK, BLK), jnp.float32),
            pltpu.VMEM((4 * WIDTH, BLK), jnp.float32),
            pltpu.VMEM((4 * WIDTH, BLK), jnp.float32),
        ],
        cost_estimate=cost(10**6, 10**3),
        compiler_params=pltpu.CompilerParams(vmem_limit_bytes=16 << 20),
        name="factor_first",
    )(mine, other)


def factor_second(state):
    return pl.pallas_call(
        second_half_kernel,
        out_shape=SQUARES,
        in_specs=[VMEM] * 3,
        out_specs=[VMEM] * 3,
        input_output_aliases={0: 0, 1: 1, 2: 2},
        scratch_shapes=[pltpu.VMEM((BLK, BLK), jnp.float32)],
        cost_estimate=cost(3 * 10**10, 10**6),
        compiler_params=pltpu.CompilerParams(vmem_limit_bytes=16 << 20),
        name="factor_second",
    )(*state)


PLACES = ((0, 0), (0, 1), (3, 0), (1, 0), (1, 1), (3, 1), (2, 0), (2, 1))


def weights_kernel(u_ref, m_ref, p0_ref, p1_ref, p2_ref, p3_ref, d_ref, own_ref, w_ref, t_ref, k_ref, p_ref):
    y, zh, core = lax.axis_index("y"), lax.axis_index("zh"), lax.axis_index("core")
    x, zl = lax.axis_index("x"), lax.axis_index("zl")
    col, row = x * 2 + zl, (y * 2 + zh) * 2 + core
    half = WIDTH // 8
    lay(t_ref, m_ref[...].T)
    arrived = [2 * ((x + dx) % 4) + (zl + dz) % 2 for dx, dz in PLACES]
    for i in range(8):
        c = 2 * ((y + 4 - i // 2) % 4) + (zh + i % 2) % 2
        k_ref[half * i : half * i + half, :] = pick(t_ref, c, 8, half, WIDTH, WIDTH)
    for i, c in enumerate(arrived):
        p_ref[half * i : half * i + half, :] = pick(t_ref, c, 8, half, WIDTH, WIDTH)
    top = jnp.concatenate(
        [ref[i] for ref in (p0_ref, p1_ref, p2_ref, p3_ref) for i in range(2)], axis=0
    )
    solved = dot(top, k_ref[...], 0, 0)
    w_ref[...] = dot(solved, p_ref[...], 1, 1)
    lay(t_ref, m_ref[...])
    mine = pick(t_ref, col, 8, half, WIDTH, WIDTH)
    lay(t_ref, u_ref[...])
    both = jnp.concatenate([mine, pick(t_ref, col, 8, half, WIDTH, WIDTH)], axis=0).T
    t_ref[:WIDTH, :] = both
    own = jnp.concatenate([t_ref[pl.ds(c, half, stride=8), :] for c in arrived], axis=0)
    own_ref[...] = own[:, :half].T
    d_ref[...] = t_ref[pl.ds(row, WIDTH // 16, stride=16), :][:, half:]


def make_weights(upper, inverse, pairs):
    return pl.pallas_call(
        weights_kernel,
        out_shape=[
            jax.ShapeDtypeStruct((WIDTH // 16, WIDTH // 8), jnp.float32),
            jax.ShapeDtypeStruct((WIDTH // 8, WIDTH), jnp.float32),
            jax.ShapeDtypeStruct((pairs[0].shape[2], WIDTH), jnp.float32),
        ],
        in_specs=[VMEM] * 6,
        out_specs=[VMEM] * 3,
        scratch_shapes=[pltpu.VMEM((4 * WIDTH, BLK), jnp.float32)]
        + [pltpu.VMEM((WIDTH, WIDTH), jnp.float32)] * 2,
        cost_estimate=cost(10**6, 10**3),
        compiler_params=pltpu.CompilerParams(vmem_limit_bytes=24 << 20),
        name="weights",
    )(upper, inverse, *pairs)


def split(a):
    high = a.astype(jnp.bfloat16)
    return high, (a - high.astype(jnp.float32)).astype(jnp.bfloat16)


def thrice(a, b, ca, cb):
    (ah, al), (bh, bl) = a, b
    return dot(ah, bh, ca, cb, None) + dot(ah, bl, ca, cb, None) + dot(al, bh, ca, cb, None)


def subtract(place, own, high, low, blocks, trail_ref, pf, pf_ref, out_ref):
    part = jnp.concatenate([ref[...] for ref in blocks], axis=0)
    at = slice(WIDTH // 8 * place, WIDTH // 8 * place + part.shape[0])
    mine = thrice(split(own[:, at]), split(part), 1, 0)
    pf_ref[...] = mine if pf is None else pf[...] + mine
    (ah, al), bh, bl = split(part.T), high[at, :], low[at, :]
    if 3 * part.shape[0] <= 256:
        change = dot(
            jnp.concatenate([ah, al, ah], axis=1), jnp.concatenate([bh, bh, bl], axis=0), 1, 0, None
        )
    else:
        change = thrice((ah, al), (bh, bl), 1, 0)
    out_ref[...] = trail_ref[...] - change


def start_kernel(mine_ref, other_ref, own_ref, *refs):
    blocks, (trail_ref, pf_ref, out_ref, high_ref, low_ref, w_ref) = refs[:-6], refs[-6:]

    @pl.when(pl.program_id(0) == 0)
    def _():
        core = lax.axis_index("core")
        n = mine_ref.shape[0]
        fill(w_ref, core, 2, mine_ref[...])
        fill(w_ref, 1 - core, 2, other_ref[...])
        for i in range(WIDTH // BLK):
            at = slice(BLK * i, BLK * i + BLK)
            high_ref[at, :], low_ref[at, :] = split(w_ref[2 * n * i : 2 * n * i + 2 * n, :].T)

    subtract(0, own_ref[...], high_ref, low_ref, blocks, trail_ref, None, pf_ref, out_ref)


def go_on_kernel(own_ref, high_ref, low_ref, *refs, place):
    blocks, (pf_in_ref, trail_ref, pf_ref, out_ref) = refs[:-4], refs[-4:]
    subtract(place, own_ref[...], high_ref, low_ref, blocks, trail_ref, pf_in_ref, pf_ref, out_ref)


def whole(shape):
    return pl.BlockSpec(shape, lambda i: (0, 0))


def update_start(mine, other, own, blocks, trailing, tile=512):
    rows, columns = trailing.shape
    lanes = pl.BlockSpec((WIDTH // 8, tile), lambda i: (0, i))
    wide = pl.BlockSpec((tile, columns), lambda i: (i, 0))
    return pl.pallas_call(
        start_kernel,
        grid=(rows // tile,),
        out_shape=[
            jax.ShapeDtypeStruct((WIDTH // 8, rows), jnp.float32),
            jax.ShapeDtypeStruct((rows, columns), jnp.float32),
        ]
        + [jax.ShapeDtypeStruct((WIDTH, columns), jnp.bfloat16)] * 2,
        in_specs=[whole(mine.shape), whole(other.shape), whole(own.shape)] + [lanes] * len(blocks)
        + [wide],
        out_specs=[lanes, wide] + [whole((WIDTH, columns))] * 2,
        scratch_shapes=[pltpu.VMEM((columns * WIDTH // BLK, BLK), jnp.float32)],
        cost_estimate=cost(8 * 10**9, 10**7),
        compiler_params=pltpu.CompilerParams(vmem_limit_bytes=24 << 20),
        name="update_start",
    )(mine, other, own, *blocks, trailing)


def update_more(place, own, high, low, blocks, pf, trailing, tile, name):
    rows, columns = trailing.shape
    lanes = pl.BlockSpec((WIDTH // 8, tile), lambda i: (0, i))
    wide = pl.BlockSpec((tile, columns), lambda i: (i, 0))
    return pl.pallas_call(
        functools.partial(go_on_kernel, place=place),
        grid=(rows // tile,),
        out_shape=[
            jax.ShapeDtypeStruct((WIDTH // 8, rows), jnp.float32),
            jax.ShapeDtypeStruct((rows, columns), jnp.float32),
        ],
        in_specs=[whole(own.shape), whole(high.shape), whole(low.shape)]
        + [lanes] * (len(blocks) + 1)
        + [wide],
        out_specs=[lanes, wide],
        cost_estimate=cost(10**9 * len(blocks), 10**7),
        compiler_params=pltpu.CompilerParams(vmem_limit_bytes=24 << 20),
        name=name,
    )(own, high, low, *blocks, pf, trailing)


def ring(n, step):
    return [(i, (i + step) % n) for i in range(n)]


def shift(x, axis, step):
    return lax.ppermute(x, axis, ring(lax.axis_size(axis), step))


def order(*arrays):
    return lax.optimization_barrier(arrays)


def gather_tiles(tile):
    half = tile.shape[0] // 2
    flat = jnp.concatenate([tile[:half], tile[half:]], axis=1)
    return lax.all_to_all(
        jnp.broadcast_to(flat[None], (64,) + flat.shape), ("y", "zh", "x", "zl"), 0, 0, tiled=True
    )


def top_moves(flip):
    moves = []
    for source in range(128):
        y, zh, core, x, zl = (source // s % n for s, n in ((32, 4), (16, 2), (8, 2), (2, 4), (1, 2)))
        target = (((x * 2 + (zl + flip) % 2) * 2 + y // 2) * 4 + 2 * (y % 2) + zh) * 2 + core
        moves.append((source, target))
    return moves


def shards(diag_block, panel_below, trailing):
    panel_t = panel_below.T
    top_len = trailing.shape[1] // 2
    mine = gather_tiles(diag_block)
    from_z = shift(panel_t, "zl", 1)
    from_l = shift(panel_t, "x", 1)
    from_r = shift(panel_t, "x", -1)
    everything = ("y", "zh", "core", "x", "zl")
    raw = panel_t[:, :top_len]
    pieces = [lax.ppermute(raw, everything, top_moves(flip)) for flip in (0, 1)]
    other = shift(mine, "core", 1)
    state = factor_first(mine, other)
    *state, from_z, from_l, from_r = order(*state, from_z, from_l, from_r)
    from_rz = shift(from_r, "zl", 1)
    from_lz = shift(from_z, "x", 1)
    from_2 = shift(from_r, "x", -1)
    _, upper, inverse = factor_second(state)
    upper, inverse, *pieces = order(upper, inverse, *pieces)
    pair = jnp.stack(pieces)
    pairs = [pair] + [shift(pair, "y", s) for s in (1, 2, 3)]
    upper, inverse, from_rz, from_lz, from_2, *pairs = order(
        upper, inverse, from_rz, from_lz, from_2, *pairs
    )
    diag_factor, own, weights = make_weights(upper, inverse, pairs)
    third = panel_t.shape[1] // 3
    parts = (
        shift(from_2[:, :third], "zl", 1),
        shift(from_lz[:, third : 2 * third], "x", 1),
        shift(from_rz[:, 2 * third :], "x", -1),
    )
    weights_other = shift(weights, "core", 1)
    blocks = [panel_t, from_z, from_l, from_r, from_rz, from_lz, from_2]
    factor_part, rest, high, low = update_start(weights, weights_other, own, blocks, trailing)
    factor_part, rest, *parts = order(factor_part, rest, *parts)
    from_2z = jnp.concatenate(parts, axis=1)
    panel_factor, new_trailing = update_more(
        7, own, high, low, [from_2z], factor_part, rest, 1024, "update_last"
    )
    return (diag_factor, panel_factor.T, new_trailing)


def solution(mesh):
    fine = Mesh(mesh.devices.reshape(4, 2, 2, 4, 2), ("y", "zh", "core", "x", "zl"))
    spec = P(("y", "zh", "core"), ("x", "zl"))
    return jax.shard_map(
        shards, mesh=fine, in_specs=(spec,) * 3, out_specs=(spec,) * 3, check_vma=False
    )
```

```python
import functools

import jax
import jax.numpy as jnp
from jax import lax
from jax.experimental import pallas as pl
from jax.experimental.pallas import tpu as pltpu
from jax.sharding import Mesh
from jax.sharding import PartitionSpec as P

HI = lax.Precision.HIGHEST
WIDTH = 512
BLK = 128
SUB = 8


def dot(a, b, ca, cb, precision=HI):
    return lax.dot_general(
        a, b, (((ca,), (cb,)), ((), ())), precision=precision, preferred_element_type=jnp.float32
    )


def lanes_of(x, k):
    return jnp.broadcast_to(x[:, k : k + 1], (SUB, BLK))


def row_of(x, j):
    return jnp.broadcast_to(x[j : j + 1, :], (SUB, BLK))


def eliminate_strip(rows, first):
    lane = lax.broadcasted_iota(jnp.int32, (SUB, BLK), 1)
    sub = lax.broadcasted_iota(jnp.int32, (SUB, BLK), 0)
    rows, scales, ahead = list(rows), [], None
    for b in range(len(rows)):
        base = SUB * (first + b)
        cols = {
            i: [lanes_of(rows[i], base + k) for k in range(SUB)]
            for i in range(b, len(rows))
            if i > b or ahead is None
        }
        if ahead is not None:
            cols[b] = ahead
        if b + 1 < len(rows):
            ahead = [lanes_of(rows[b + 1], base + SUB + k) for k in range(SUB)]
        scale = jnp.zeros((SUB, BLK), jnp.float32)
        for j in range(SUB):
            pivot_row = {k: row_of(cols[b][k], j) for k in range(j, SUB)}
            at = lane == base + j
            wide = jnp.where(at, 1.0, row_of(rows[b], j))
            inv = 1.0 / pivot_row[j]
            scale = jnp.where(sub == j, lax.rsqrt(pivot_row[j]), scale)
            for i in range(b, len(rows)):
                m = cols[i][j] * inv
                here = at
                if i == b:
                    m = jnp.where(sub > j, m, 0.0)
                    here = at & (sub > j)
                if i == b + 1:
                    for k in range(SUB):
                        ahead[k] = ahead[k] - m * row_of(cols[i][j], k)
                for k in range(j + 1, SUB):
                    cols[i][k] = cols[i][k] - m * pivot_row[k]
                rows[i] = jnp.where(here, 0.0, rows[i]) - m * wide
        rows[b] = rows[b] * scale
        scales.append(scale)
    return rows, scales


def eliminate(rows, strip=8):
    lane = lax.broadcasted_iota(jnp.int32, (SUB, BLK), 1)
    sub = lax.broadcasted_iota(jnp.int32, (SUB, BLK), 0)
    rows, scales = list(rows), []
    for s in range(0, len(rows), strip):
        e = s + strip
        rows[s:e], found = eliminate_strip(rows[s:e], s)
        scales += found
        if e < len(rows):
            inside = (lane >= SUB * s) & (lane < SUB * e)
            own = [
                jnp.where(
                    inside & (lane >= sub + SUB * i),
                    jnp.where(lane == sub + SUB * i, scales[i], 0.0),
                    rows[i],
                )
                for i in range(s, e)
            ]
            change = dot(jnp.concatenate(rows[s:e], axis=0), jnp.concatenate(own, axis=0), 0, 0)
            for i in range(e, len(rows)):
                rows[i] = jnp.where(inside, 0.0, rows[i]) - change[SUB * i : SUB * i + SUB]
    return rows, scales


def fill(tall_ref, start, stride, value):
    rows, columns = value.shape
    height = tall_ref.shape[0] * BLK // columns
    for i in range(columns // BLK):
        tall_ref[pl.ds(i * height + start, rows, stride=stride), :] = value[:, BLK * i : BLK * i + BLK]


def pick(tall_ref, start, stride, rows, columns, height):
    return jnp.concatenate(
        [
            tall_ref[pl.ds(i * height + start, rows, stride=stride), :]
            for i in range(columns // BLK)
        ],
        axis=1,
    )


def lay(tall_ref, value):
    height = value.shape[0]
    for i in range(value.shape[1] // BLK):
        tall_ref[i * height : i * height + height, :] = value[:, BLK * i : BLK * i + BLK]


def assemble(mine_ref, other_ref, wide_ref, tall_ref, a_ref):
    core = lax.axis_index("core")
    left = lax.broadcasted_iota(jnp.int32, (16, BLK), 1) < BLK // 2
    for ref, start in ((mine_ref, core), (other_ref, 1 - core)):
        for yz in range(8):
            for x in range(4):
                one, two = ref[yz * 8 + 2 * x], ref[yz * 8 + 2 * x + 1]
                upper = jnp.where(left, one, pltpu.roll(two, BLK // 2, 1))
                lower = jnp.where(left, pltpu.roll(one, BLK // 2, 1), two)
                at = x * WIDTH + yz * 2 + start
                wide_ref[pl.ds(at, 16, stride=16), :] = upper
                wide_ref[pl.ds(at + WIDTH // 2, 16, stride=16), :] = lower
    for x in range(4):
        turned = wide_ref[x * WIDTH : x * WIDTH + WIDTH, :].T
        fill(tall_ref, 2 * x, 8, turned[:64])
        fill(tall_ref, 2 * x + 1, 8, turned[64:])
    for i in range(4):
        a_ref[:, BLK * i : BLK * i + BLK] = tall_ref[i * WIDTH : i * WIDTH + WIDTH, :]


def factor_steps(offsets, r_ref, u_ref, m_ref, t_ref):
    lane = lax.broadcasted_iota(jnp.int32, (SUB, BLK), 1)
    sub = lax.broadcasted_iota(jnp.int32, (SUB, BLK), 0)
    for o in offsets:
        e = o + BLK
        rows = [r_ref[o + i : o + i + SUB, o:e] for i in range(0, BLK, SUB)]
        rows, scales = eliminate(rows)
        for i in range(BLK // SUB):
            at = sub + SUB * i
            u_ref[o + SUB * i : o + SUB * i + SUB, o:e] = jnp.where(lane >= at, rows[i], 0.0)
            t_ref[SUB * i : SUB * i + SUB, :] = jnp.where(
                lane < at, rows[i], jnp.where(lane == at, scales[i], 0.0)
            )
        inv = t_ref[...]
        m_ref[o:e, o:e] = inv
        if o:
            m_ref[o:e, :o] = dot(inv, r_ref[o:e, :o], 1, 0)
        if e < WIDTH:
            u = dot(inv, r_ref[o:e, e:], 1, 0)
            u_ref[o:e, e:] = u
            r_ref[e:, e:] = r_ref[e:, e:] - dot(u, u, 0, 0)
            z = dot(u, m_ref[o:e, :e], 0, 0)
            if o:
                r_ref[e:, :o] = r_ref[e:, :o] - z[:, :o]
            r_ref[e:, o:e] = -z[:, o:]


def first_half_kernel(mine_ref, other_ref, r_ref, u_ref, m_ref, t_ref, wide_ref, tall_ref):
    assemble(mine_ref, other_ref, wide_ref, tall_ref, r_ref)
    u_ref[...] = jnp.zeros_like(u_ref)
    m_ref[...] = jnp.zeros_like(m_ref)
    factor_steps((0, BLK), r_ref, u_ref, m_ref, t_ref)


def second_half_kernel(r_in, u_in, m_in, r_ref, u_ref, m_ref, t_ref):
    del r_in, u_in, m_in
    factor_steps((2 * BLK, 3 * BLK), r_ref, u_ref, m_ref, t_ref)


VMEM = pl.BlockSpec(memory_space=pltpu.VMEM)


def cost(flops, bytes_accessed):
    return pl.CostEstimate(flops=flops, bytes_accessed=bytes_accessed, transcendentals=0)


SQUARES = [jax.ShapeDtypeStruct((WIDTH, WIDTH), jnp.float32)] * 3


def factor_first(mine, other):
    return pl.pallas_call(
        first_half_kernel,
        out_shape=SQUARES,
        in_specs=[VMEM] * 2,
        out_specs=[VMEM] * 3,
        scratch_shapes=[
            pltpu.VMEM((BLK, BLK), jnp.float32),
            pltpu.VMEM((4 * WIDTH, BLK), jnp.float32),
            pltpu.VMEM((4 * WIDTH, BLK), jnp.float32),
        ],
        cost_estimate=cost(10**6, 10**3),
        compiler_params=pltpu.CompilerParams(vmem_limit_bytes=16 << 20),
        name="factor_first",
    )(mine, other)


def factor_second(state):
    return pl.pallas_call(
        second_half_kernel,
        out_shape=SQUARES,
        in_specs=[VMEM] * 3,
        out_specs=[VMEM] * 3,
        input_output_aliases={0: 0, 1: 1, 2: 2},
        scratch_shapes=[pltpu.VMEM((BLK, BLK), jnp.float32)],
        cost_estimate=cost(3 * 10**10, 10**6),
        compiler_params=pltpu.CompilerParams(vmem_limit_bytes=16 << 20),
        name="factor_second",
    )(*state)


PLACES = ((0, 0), (0, 1), (3, 0), (1, 0), (1, 1), (3, 1), (2, 0), (2, 1))


def weights_kernel(u_ref, m_ref, p0_ref, p1_ref, p2_ref, p3_ref, d_ref, own_ref, w_ref, t_ref, k_ref, p_ref):
    y, zh, core = lax.axis_index("y"), lax.axis_index("zh"), lax.axis_index("core")
    x, zl = lax.axis_index("x"), lax.axis_index("zl")
    col, row = x * 2 + zl, (y * 2 + zh) * 2 + core
    half = WIDTH // 8
    lay(t_ref, m_ref[...].T)
    arrived = [2 * ((x + dx) % 4) + (zl + dz) % 2 for dx, dz in PLACES]
    for i in range(8):
        c = 2 * ((y + 4 - i // 2) % 4) + (zh + i % 2) % 2
        k_ref[half * i : half * i + half, :] = pick(t_ref, c, 8, half, WIDTH, WIDTH)
    for i, c in enumerate(arrived):
        p_ref[half * i : half * i + half, :] = pick(t_ref, c, 8, half, WIDTH, WIDTH)
    top = jnp.concatenate(
        [ref[i] for ref in (p0_ref, p1_ref, p2_ref, p3_ref) for i in range(2)], axis=0
    )
    solved = thrice(split(top.T), split(k_ref[...]), 1, 0)
    w_ref[...] = thrice(split(solved), split(p_ref[...]), 1, 1)
    lay(t_ref, m_ref[...])
    mine = pick(t_ref, col, 8, half, WIDTH, WIDTH)
    lay(t_ref, u_ref[...])
    both = jnp.concatenate([mine, pick(t_ref, col, 8, half, WIDTH, WIDTH)], axis=0).T
    t_ref[:WIDTH, :] = both
    own = jnp.concatenate([t_ref[pl.ds(c, half, stride=8), :] for c in arrived], axis=0)
    own_ref[...] = own[:, :half].T
    d_ref[...] = t_ref[pl.ds(row, WIDTH // 16, stride=16), :][:, half:]


def make_weights(upper, inverse, pairs):
    return pl.pallas_call(
        weights_kernel,
        out_shape=[
            jax.ShapeDtypeStruct((WIDTH // 16, WIDTH // 8), jnp.float32),
            jax.ShapeDtypeStruct((WIDTH // 8, WIDTH), jnp.float32),
            jax.ShapeDtypeStruct((pairs[0].shape[2], WIDTH), jnp.float32),
        ],
        in_specs=[VMEM] * 6,
        out_specs=[VMEM] * 3,
        scratch_shapes=[pltpu.VMEM((4 * WIDTH, BLK), jnp.float32)]
        + [pltpu.VMEM((WIDTH, WIDTH), jnp.float32)] * 2,
        cost_estimate=cost(10**6, 10**3),
        compiler_params=pltpu.CompilerParams(vmem_limit_bytes=24 << 20),
        name="weights",
    )(upper, inverse, *pairs)


def split(a):
    high = a.astype(jnp.bfloat16)
    return high, (a - high.astype(jnp.float32)).astype(jnp.bfloat16)


def thrice(a, b, ca, cb):
    (ah, al), (bh, bl) = a, b
    return dot(ah, bh, ca, cb, None) + dot(ah, bl, ca, cb, None) + dot(al, bh, ca, cb, None)


def subtract(place, own, high, low, blocks, trail_ref, pf, pf_ref, out_ref):
    part = jnp.concatenate([ref[...] for ref in blocks], axis=0)
    at = slice(WIDTH // 8 * place, WIDTH // 8 * place + part.shape[0])
    mine = thrice(split(own[:, at]), split(part), 1, 0)
    pf_ref[...] = mine if pf is None else pf[...] + mine
    (ah, al), bh, bl = split(part.T), high[at, :], low[at, :]
    if 3 * part.shape[0] <= 256:
        change = dot(
            jnp.concatenate([ah, al, ah], axis=1), jnp.concatenate([bh, bh, bl], axis=0), 1, 0, None
        )
    else:
        change = thrice((ah, al), (bh, bl), 1, 0)
    out_ref[...] = trail_ref[...] - change


def start_kernel(mine_ref, other_ref, own_ref, *refs):
    blocks, (trail_ref, pf_ref, out_ref, high_ref, low_ref, w_ref) = refs[:-6], refs[-6:]

    @pl.when(pl.program_id(0) == 0)
    def _():
        core = lax.axis_index("core")
        n = mine_ref.shape[0]
        fill(w_ref, core, 2, mine_ref[...])
        fill(w_ref, 1 - core, 2, other_ref[...])
        for i in range(WIDTH // BLK):
            at = slice(BLK * i, BLK * i + BLK)
            high_ref[at, :], low_ref[at, :] = split(w_ref[2 * n * i : 2 * n * i + 2 * n, :].T)

    subtract(0, own_ref[...], high_ref, low_ref, blocks, trail_ref, None, pf_ref, out_ref)


def go_on_kernel(own_ref, high_ref, low_ref, *refs, place):
    blocks, (pf_in_ref, trail_ref, pf_ref, out_ref) = refs[:-4], refs[-4:]
    subtract(place, own_ref[...], high_ref, low_ref, blocks, trail_ref, pf_in_ref, pf_ref, out_ref)


def whole(shape):
    return pl.BlockSpec(shape, lambda i: (0, 0))


def update_start(mine, other, own, blocks, trailing, tile=512):
    rows, columns = trailing.shape
    lanes = pl.BlockSpec((WIDTH // 8, tile), lambda i: (0, i))
    wide = pl.BlockSpec((tile, columns), lambda i: (i, 0))
    return pl.pallas_call(
        start_kernel,
        grid=(rows // tile,),
        out_shape=[
            jax.ShapeDtypeStruct((WIDTH // 8, rows), jnp.float32),
            jax.ShapeDtypeStruct((rows, columns), jnp.float32),
        ]
        + [jax.ShapeDtypeStruct((WIDTH, columns), jnp.bfloat16)] * 2,
        in_specs=[whole(mine.shape), whole(other.shape), whole(own.shape)] + [lanes] * len(blocks)
        + [wide],
        out_specs=[lanes, wide] + [whole((WIDTH, columns))] * 2,
        scratch_shapes=[pltpu.VMEM((columns * WIDTH // BLK, BLK), jnp.float32)],
        cost_estimate=cost(8 * 10**9, 10**7),
        compiler_params=pltpu.CompilerParams(vmem_limit_bytes=24 << 20),
        name="update_start",
    )(mine, other, own, *blocks, trailing)


def update_more(place, own, high, low, blocks, pf, trailing, tile, name):
    rows, columns = trailing.shape
    lanes = pl.BlockSpec((WIDTH // 8, tile), lambda i: (0, i))
    wide = pl.BlockSpec((tile, columns), lambda i: (i, 0))
    return pl.pallas_call(
        functools.partial(go_on_kernel, place=place),
        grid=(rows // tile,),
        out_shape=[
            jax.ShapeDtypeStruct((WIDTH // 8, rows), jnp.float32),
            jax.ShapeDtypeStruct((rows, columns), jnp.float32),
        ],
        in_specs=[whole(own.shape), whole(high.shape), whole(low.shape)]
        + [lanes] * (len(blocks) + 1)
        + [wide],
        out_specs=[lanes, wide],
        cost_estimate=cost(10**9 * len(blocks), 10**7),
        compiler_params=pltpu.CompilerParams(vmem_limit_bytes=24 << 20),
        name=name,
    )(own, high, low, *blocks, pf, trailing)


def ring(n, step):
    return [(i, (i + step) % n) for i in range(n)]


def shift(x, axis, step):
    return lax.ppermute(x, axis, ring(lax.axis_size(axis), step))


def order(*arrays):
    return lax.optimization_barrier(arrays)


def gather_tiles(tile):
    half = tile.shape[0] // 2
    flat = jnp.concatenate([tile[:half], tile[half:]], axis=1)
    return lax.all_to_all(
        jnp.broadcast_to(flat[None], (64,) + flat.shape), ("y", "zh", "x", "zl"), 0, 0, tiled=True
    )


def top_moves(flip):
    moves = []
    for source in range(128):
        y, zh, core, x, zl = (source // s % n for s, n in ((32, 4), (16, 2), (8, 2), (2, 4), (1, 2)))
        target = (((x * 2 + (zl + flip) % 2) * 2 + y // 2) * 4 + 2 * (y % 2) + zh) * 2 + core
        moves.append((source, target))
    return moves


def shards(diag_block, panel_below, trailing):
    panel_t = panel_below.T
    top_len = trailing.shape[1] // 2
    mine = gather_tiles(diag_block)
    from_z = shift(panel_t, "zl", 1)
    from_l = shift(panel_t, "x", 1)
    from_r = shift(panel_t, "x", -1)
    everything = ("y", "zh", "core", "x", "zl")
    raw = panel_t[:, :top_len]
    pieces = [lax.ppermute(raw, everything, top_moves(flip)) for flip in (0, 1)]
    other = shift(mine, "core", 1)
    state = factor_first(mine, other)
    *state, from_z, from_l, from_r = order(*state, from_z, from_l, from_r)
    from_rz = shift(from_r, "zl", 1)
    from_lz = shift(from_z, "x", 1)
    from_2 = shift(from_r, "x", -1)
    _, upper, inverse = factor_second(state)
    upper, inverse, *pieces = order(upper, inverse, *pieces)
    pair = jnp.stack(pieces)
    pairs = [pair] + [shift(pair, "y", s) for s in (1, 2, 3)]
    upper, inverse, from_rz, from_lz, from_2, *pairs = order(
        upper, inverse, from_rz, from_lz, from_2, *pairs
    )
    diag_factor, own, weights = make_weights(upper, inverse, pairs)
    third = panel_t.shape[1] // 3
    parts = (
        shift(from_2[:, :third], "zl", 1),
        shift(from_lz[:, third : 2 * third], "x", 1),
        shift(from_rz[:, 2 * third :], "x", -1),
    )
    weights_other = shift(weights, "core", 1)
    blocks = [panel_t, from_z, from_l, from_r, from_rz, from_lz, from_2]
    factor_part, rest, high, low = update_start(weights, weights_other, own, blocks, trailing)
    factor_part, rest, *parts = order(factor_part, rest, *parts)
    from_2z = jnp.concatenate(parts, axis=1)
    panel_factor, new_trailing = update_more(
        7, own, high, low, [from_2z], factor_part, rest, 1024, "update_last"
    )
    return (diag_factor, panel_factor.T, new_trailing)


def solution(mesh):
    fine = Mesh(mesh.devices.reshape(4, 2, 2, 4, 2), ("y", "zh", "core", "x", "zl"))
    spec = P(("y", "zh", "core"), ("x", "zl"))
    return jax.shard_map(
        shards, mesh=fine, in_specs=(spec,) * 3, out_specs=(spec,) * 3, check_vma=False
    )
```

```python
import functools

import jax
import jax.numpy as jnp
from jax import lax
from jax.experimental import pallas as pl
from jax.experimental.pallas import tpu as pltpu
from jax.sharding import Mesh
from jax.sharding import PartitionSpec as P

HI = lax.Precision.HIGHEST
WIDTH = 512
BLK = 128
SUB = 8


def dot(a, b, ca, cb, precision=HI):
    return lax.dot_general(
        a, b, (((ca,), (cb,)), ((), ())), precision=precision, preferred_element_type=jnp.float32
    )


def lanes_of(x, k):
    return jnp.broadcast_to(x[:, k : k + 1], (SUB, BLK))


def row_of(x, j):
    return jnp.broadcast_to(x[j : j + 1, :], (SUB, BLK))


def eliminate_strip(rows, first):
    lane = lax.broadcasted_iota(jnp.int32, (SUB, BLK), 1)
    sub = lax.broadcasted_iota(jnp.int32, (SUB, BLK), 0)
    rows, scales, ahead = list(rows), [], None
    for b in range(len(rows)):
        base = SUB * (first + b)
        cols = {
            i: [lanes_of(rows[i], base + k) for k in range(SUB)]
            for i in range(b, len(rows))
            if i > b or ahead is None
        }
        if ahead is not None:
            cols[b] = ahead
        if b + 1 < len(rows):
            ahead = [lanes_of(rows[b + 1], base + SUB + k) for k in range(SUB)]
        scale = jnp.zeros((SUB, BLK), jnp.float32)
        for j in range(SUB):
            pivot_row = {k: row_of(cols[b][k], j) for k in range(j, SUB)}
            at = lane == base + j
            wide = jnp.where(at, 1.0, row_of(rows[b], j))
            inv = 1.0 / pivot_row[j]
            scale = jnp.where(sub == j, lax.rsqrt(pivot_row[j]), scale)
            for i in range(b, len(rows)):
                m = cols[i][j] * inv
                here = at
                if i == b:
                    m = jnp.where(sub > j, m, 0.0)
                    here = at & (sub > j)
                if i == b + 1:
                    for k in range(SUB):
                        ahead[k] = ahead[k] - m * row_of(cols[i][j], k)
                for k in range(j + 1, SUB):
                    cols[i][k] = cols[i][k] - m * pivot_row[k]
                rows[i] = jnp.where(here, 0.0, rows[i]) - m * wide
        rows[b] = rows[b] * scale
        scales.append(scale)
    return rows, scales


def eliminate(rows, strip=8):
    lane = lax.broadcasted_iota(jnp.int32, (SUB, BLK), 1)
    sub = lax.broadcasted_iota(jnp.int32, (SUB, BLK), 0)
    rows, scales = list(rows), []
    for s in range(0, len(rows), strip):
        e = s + strip
        rows[s:e], found = eliminate_strip(rows[s:e], s)
        scales += found
        if e < len(rows):
            inside = (lane >= SUB * s) & (lane < SUB * e)
            own = [
                jnp.where(
                    inside & (lane >= sub + SUB * i),
                    jnp.where(lane == sub + SUB * i, scales[i], 0.0),
                    rows[i],
                )
                for i in range(s, e)
            ]
            change = dot(jnp.concatenate(rows[s:e], axis=0), jnp.concatenate(own, axis=0), 0, 0)
            for i in range(e, len(rows)):
                rows[i] = jnp.where(inside, 0.0, rows[i]) - change[SUB * i : SUB * i + SUB]
    return rows, scales


def fill(tall_ref, start, stride, value):
    rows, columns = value.shape
    height = tall_ref.shape[0] * BLK // columns
    for i in range(columns // BLK):
        tall_ref[pl.ds(i * height + start, rows, stride=stride), :] = value[:, BLK * i : BLK * i + BLK]


def pick(tall_ref, start, stride, rows, columns, height):
    return jnp.concatenate(
        [
            tall_ref[pl.ds(i * height + start, rows, stride=stride), :]
            for i in range(columns // BLK)
        ],
        axis=1,
    )


def lay(tall_ref, value):
    height = value.shape[0]
    for i in range(value.shape[1] // BLK):
        tall_ref[i * height : i * height + height, :] = value[:, BLK * i : BLK * i + BLK]


def assemble(mine_ref, other_ref, wide_ref, tall_ref, a_ref):
    core = lax.axis_index("core")
    left = lax.broadcasted_iota(jnp.int32, (16, BLK), 1) < BLK // 2
    for ref, start in ((mine_ref, core), (other_ref, 1 - core)):
        for yz in range(8):
            for x in range(4):
                one, two = ref[yz * 8 + 2 * x], ref[yz * 8 + 2 * x + 1]
                upper = jnp.where(left, one, pltpu.roll(two, BLK // 2, 1))
                lower = jnp.where(left, pltpu.roll(one, BLK // 2, 1), two)
                at = x * WIDTH + yz * 2 + start
                wide_ref[pl.ds(at, 16, stride=16), :] = upper
                wide_ref[pl.ds(at + WIDTH // 2, 16, stride=16), :] = lower
    for x in range(4):
        turned = wide_ref[x * WIDTH : x * WIDTH + WIDTH, :].T
        fill(tall_ref, 2 * x, 8, turned[:64])
        fill(tall_ref, 2 * x + 1, 8, turned[64:])
    for i in range(4):
        a_ref[:, BLK * i : BLK * i + BLK] = tall_ref[i * WIDTH : i * WIDTH + WIDTH, :]


def factor_steps(offsets, r_ref, u_ref, m_ref, t_ref):
    lane = lax.broadcasted_iota(jnp.int32, (SUB, BLK), 1)
    sub = lax.broadcasted_iota(jnp.int32, (SUB, BLK), 0)
    for o in offsets:
        e = o + BLK
        rows = [r_ref[o + i : o + i + SUB, o:e] for i in range(0, BLK, SUB)]
        rows, scales = eliminate(rows)
        for i in range(BLK // SUB):
            at = sub + SUB * i
            u_ref[o + SUB * i : o + SUB * i + SUB, o:e] = jnp.where(lane >= at, rows[i], 0.0)
            t_ref[SUB * i : SUB * i + SUB, :] = jnp.where(
                lane < at, rows[i], jnp.where(lane == at, scales[i], 0.0)
            )
        inv = t_ref[...]
        m_ref[o:e, o:e] = inv
        if o:
            m_ref[o:e, :o] = dot(inv, r_ref[o:e, :o], 1, 0)
        if e < WIDTH:
            u = dot(inv, r_ref[o:e, e:], 1, 0)
            u_ref[o:e, e:] = u
            r_ref[e:, e:] = r_ref[e:, e:] - dot(u, u, 0, 0)
            z = dot(u, m_ref[o:e, :e], 0, 0)
            if o:
                r_ref[e:, :o] = r_ref[e:, :o] - z[:, :o]
            r_ref[e:, o:e] = -z[:, o:]


def first_half_kernel(mine_ref, other_ref, r_ref, u_ref, m_ref, t_ref, wide_ref, tall_ref):
    assemble(mine_ref, other_ref, wide_ref, tall_ref, r_ref)
    u_ref[...] = jnp.zeros_like(u_ref)
    m_ref[...] = jnp.zeros_like(m_ref)
    factor_steps((0, BLK), r_ref, u_ref, m_ref, t_ref)


def second_half_kernel(r_in, u_in, m_in, r_ref, u_ref, m_ref, t_ref):
    del r_in, u_in, m_in
    factor_steps((2 * BLK, 3 * BLK), r_ref, u_ref, m_ref, t_ref)


VMEM = pl.BlockSpec(memory_space=pltpu.VMEM)


def cost(flops, bytes_accessed):
    return pl.CostEstimate(flops=flops, bytes_accessed=bytes_accessed, transcendentals=0)


SQUARES = [jax.ShapeDtypeStruct((WIDTH, WIDTH), jnp.float32)] * 3


def factor_first(mine, other):
    return pl.pallas_call(
        first_half_kernel,
        out_shape=SQUARES,
        in_specs=[VMEM] * 2,
        out_specs=[VMEM] * 3,
        scratch_shapes=[
            pltpu.VMEM((BLK, BLK), jnp.float32),
            pltpu.VMEM((4 * WIDTH, BLK), jnp.float32),
            pltpu.VMEM((4 * WIDTH, BLK), jnp.float32),
        ],
        cost_estimate=cost(10**6, 10**3),
        compiler_params=pltpu.CompilerParams(vmem_limit_bytes=16 << 20),
        name="factor_first",
    )(mine, other)


def factor_second(state):
    return pl.pallas_call(
        second_half_kernel,
        out_shape=SQUARES,
        in_specs=[VMEM] * 3,
        out_specs=[VMEM] * 3,
        input_output_aliases={0: 0, 1: 1, 2: 2},
        scratch_shapes=[pltpu.VMEM((BLK, BLK), jnp.float32)],
        cost_estimate=cost(3 * 10**10, 10**6),
        compiler_params=pltpu.CompilerParams(vmem_limit_bytes=16 << 20),
        name="factor_second",
    )(*state)


PLACES = ((0, 0), (0, 1), (3, 0), (1, 0), (1, 1), (3, 1), (2, 0), (2, 1))


def weights_kernel(u_ref, m_ref, p0_ref, p1_ref, p2_ref, p3_ref, d_ref, own_ref, w_ref, t_ref, k_ref, p_ref):
    y, zh, core = lax.axis_index("y"), lax.axis_index("zh"), lax.axis_index("core")
    x, zl = lax.axis_index("x"), lax.axis_index("zl")
    col, row = x * 2 + zl, (y * 2 + zh) * 2 + core
    half = WIDTH // 8
    lay(t_ref, m_ref[...].T)
    arrived = [2 * ((x + dx) % 4) + (zl + dz) % 2 for dx, dz in PLACES]
    for i in range(8):
        c = 2 * ((y + 4 - i // 2) % 4) + (zh + i % 2) % 2
        k_ref[half * i : half * i + half, :] = pick(t_ref, c, 8, half, WIDTH, WIDTH)
    for i, c in enumerate(arrived):
        p_ref[half * i : half * i + half, :] = pick(t_ref, c, 8, half, WIDTH, WIDTH)
    top = jnp.concatenate(
        [ref[i] for ref in (p0_ref, p1_ref, p2_ref, p3_ref) for i in range(2)], axis=0
    )
    solved = thrice(split(top.T), split(k_ref[...]), 1, 0)
    w_ref[...] = thrice(split(solved), split(p_ref[...]), 1, 1)
    lay(t_ref, m_ref[...])
    mine = pick(t_ref, col, 8, half, WIDTH, WIDTH)
    lay(t_ref, u_ref[...])
    both = jnp.concatenate([mine, pick(t_ref, col, 8, half, WIDTH, WIDTH)], axis=0).T
    t_ref[:WIDTH, :] = both
    own = jnp.concatenate([t_ref[pl.ds(c, half, stride=8), :] for c in arrived], axis=0)
    own_ref[...] = own[:, :half].T
    d_ref[...] = t_ref[pl.ds(row, WIDTH // 16, stride=16), :][:, half:]


def make_weights(upper, inverse, pairs):
    return pl.pallas_call(
        weights_kernel,
        out_shape=[
            jax.ShapeDtypeStruct((WIDTH // 16, WIDTH // 8), jnp.float32),
            jax.ShapeDtypeStruct((WIDTH // 8, WIDTH), jnp.float32),
            jax.ShapeDtypeStruct((pairs[0].shape[2], WIDTH), jnp.float32),
        ],
        in_specs=[VMEM] * 6,
        out_specs=[VMEM] * 3,
        scratch_shapes=[pltpu.VMEM((4 * WIDTH, BLK), jnp.float32)]
        + [pltpu.VMEM((WIDTH, WIDTH), jnp.float32)] * 2,
        cost_estimate=cost(10**6, 10**3),
        compiler_params=pltpu.CompilerParams(vmem_limit_bytes=24 << 20),
        name="weights",
    )(upper, inverse, *pairs)


def split(a):
    high = a.astype(jnp.bfloat16)
    return high, (a - high.astype(jnp.float32)).astype(jnp.bfloat16)


def thrice(a, b, ca, cb):
    (ah, al), (bh, bl) = a, b
    return dot(ah, bh, ca, cb, None) + dot(ah, bl, ca, cb, None) + dot(al, bh, ca, cb, None)


def subtract(place, own, high, low, blocks, trail_ref, pf, pf_ref, out_ref):
    part = jnp.concatenate([ref[...] for ref in blocks], axis=0)
    at = slice(WIDTH // 8 * place, WIDTH // 8 * place + part.shape[0])
    mine = thrice(split(own[:, at]), split(part), 1, 0)
    pf_ref[...] = mine if pf is None else pf[...] + mine
    (ah, al), bh, bl = split(part.T), high[at, :], low[at, :]
    if 3 * part.shape[0] <= 256:
        change = dot(
            jnp.concatenate([ah, al, ah], axis=1), jnp.concatenate([bh, bh, bl], axis=0), 1, 0, None
        )
    else:
        change = thrice((ah, al), (bh, bl), 1, 0)
    out_ref[...] = trail_ref[...] - change


def start_kernel(mine_ref, other_ref, own_ref, *refs):
    blocks, (trail_ref, pf_ref, out_ref, high_ref, low_ref, w_ref) = refs[:-6], refs[-6:]

    @pl.when(pl.program_id(0) == 0)
    def _():
        core = lax.axis_index("core")
        n = mine_ref.shape[0]
        fill(w_ref, core, 2, mine_ref[...])
        fill(w_ref, 1 - core, 2, other_ref[...])
        for i in range(WIDTH // BLK):
            at = slice(BLK * i, BLK * i + BLK)
            high_ref[at, :], low_ref[at, :] = split(w_ref[2 * n * i : 2 * n * i + 2 * n, :].T)

    subtract(0, own_ref[...], high_ref, low_ref, blocks, trail_ref, None, pf_ref, out_ref)


def go_on_kernel(own_ref, high_ref, low_ref, *refs, place):
    blocks, (pf_in_ref, trail_ref, pf_ref, out_ref) = refs[:-4], refs[-4:]
    subtract(place, own_ref[...], high_ref, low_ref, blocks, trail_ref, pf_in_ref, pf_ref, out_ref)


def whole(shape):
    return pl.BlockSpec(shape, lambda i: (0, 0))


def update_start(mine, other, own, blocks, trailing, tile=512):
    rows, columns = trailing.shape
    lanes = pl.BlockSpec((WIDTH // 8, tile), lambda i: (0, i))
    wide = pl.BlockSpec((tile, columns), lambda i: (i, 0))
    return pl.pallas_call(
        start_kernel,
        grid=(rows // tile,),
        out_shape=[
            jax.ShapeDtypeStruct((WIDTH // 8, rows), jnp.float32),
            jax.ShapeDtypeStruct((rows, columns), jnp.float32),
        ]
        + [jax.ShapeDtypeStruct((WIDTH, columns), jnp.bfloat16)] * 2,
        in_specs=[whole(mine.shape), whole(other.shape), whole(own.shape)] + [lanes] * len(blocks)
        + [wide],
        out_specs=[lanes, wide] + [whole((WIDTH, columns))] * 2,
        scratch_shapes=[pltpu.VMEM((columns * WIDTH // BLK, BLK), jnp.float32)],
        cost_estimate=cost(8 * 10**9, 10**7),
        compiler_params=pltpu.CompilerParams(vmem_limit_bytes=24 << 20),
        name="update_start",
    )(mine, other, own, *blocks, trailing)


def update_more(place, own, high, low, blocks, pf, trailing, tile, name):
    rows, columns = trailing.shape
    lanes = pl.BlockSpec((WIDTH // 8, tile), lambda i: (0, i))
    wide = pl.BlockSpec((tile, columns), lambda i: (i, 0))
    return pl.pallas_call(
        functools.partial(go_on_kernel, place=place),
        grid=(rows // tile,),
        out_shape=[
            jax.ShapeDtypeStruct((WIDTH // 8, rows), jnp.float32),
            jax.ShapeDtypeStruct((rows, columns), jnp.float32),
        ],
        in_specs=[whole(own.shape), whole(high.shape), whole(low.shape)]
        + [lanes] * (len(blocks) + 1)
        + [wide],
        out_specs=[lanes, wide],
        cost_estimate=cost(10**9 * len(blocks), 10**7),
        compiler_params=pltpu.CompilerParams(vmem_limit_bytes=24 << 20),
        name=name,
    )(own, high, low, *blocks, pf, trailing)


def ring(n, step):
    return [(i, (i + step) % n) for i in range(n)]


def shift(x, axis, step):
    return lax.ppermute(x, axis, ring(lax.axis_size(axis), step))


def order(*arrays):
    return lax.optimization_barrier(arrays)


def gather_tiles(tile):
    half = tile.shape[0] // 2
    flat = jnp.concatenate([tile[:half], tile[half:]], axis=1)
    return lax.all_to_all(
        jnp.broadcast_to(flat[None], (64,) + flat.shape), ("y", "zh", "x", "zl"), 0, 0, tiled=True
    )


def top_moves(flip):
    moves = []
    for source in range(128):
        y, zh, core, x, zl = (source // s % n for s, n in ((32, 4), (16, 2), (8, 2), (2, 4), (1, 2)))
        target = (((x * 2 + (zl + flip) % 2) * 2 + y // 2) * 4 + 2 * (y % 2) + zh) * 2 + core
        moves.append((source, target))
    return moves


def shards(diag_block, panel_below, trailing):
    panel_t = panel_below.T
    top_len = trailing.shape[1] // 2
    mine = gather_tiles(diag_block)
    from_z = shift(panel_t, "zl", 1)
    from_l = shift(panel_t, "x", 1)
    from_r = shift(panel_t, "x", -1)
    everything = ("y", "zh", "core", "x", "zl")
    raw = panel_t[:, :top_len]
    pieces = [lax.ppermute(raw, everything, top_moves(flip)) for flip in (0, 1)]
    other = shift(mine, "core", 1)
    state = factor_first(mine, other)
    *state, from_z, from_l, from_r = order(*state, from_z, from_l, from_r)
    from_rz = shift(from_r, "zl", 1)
    from_lz = shift(from_z, "x", 1)
    from_2 = shift(from_r, "x", -1)
    _, upper, inverse = factor_second(state)
    upper, inverse, *pieces = order(upper, inverse, *pieces)
    pair = jnp.stack(pieces)
    pairs = [pair] + [shift(pair, "y", s) for s in (1, 2, 3)]
    upper, inverse, from_rz, from_lz, from_2, *pairs = order(
        upper, inverse, from_rz, from_lz, from_2, *pairs
    )
    diag_factor, own, weights = make_weights(upper, inverse, pairs)
    half = panel_t.shape[1] // 2
    parts = (shift(from_lz[:, :half], "x", 1), shift(from_rz[:, half:], "x", -1))
    weights_other = shift(weights, "core", 1)
    blocks = [panel_t, from_z, from_l, from_r, from_rz, from_lz, from_2]
    factor_part, rest, high, low = update_start(weights, weights_other, own, blocks, trailing)
    factor_part, rest, *parts = order(factor_part, rest, *parts)
    from_2z = jnp.concatenate(parts, axis=1)
    panel_factor, new_trailing = update_more(
        7, own, high, low, [from_2z], factor_part, rest, 1024, "update_last"
    )
    return (diag_factor, panel_factor.T, new_trailing)


def solution(mesh):
    fine = Mesh(mesh.devices.reshape(4, 2, 2, 4, 2), ("y", "zh", "core", "x", "zl"))
    spec = P(("y", "zh", "core"), ("x", "zl"))
    return jax.shard_map(
        shards, mesh=fine, in_specs=(spec,) * 3, out_specs=(spec,) * 3, check_vma=False
    )
```
